32 devices in a mesh: trow: 8 (over y, x, core), tcol: 4 (over z).
Axes of the slice: x: 2, y: 2, z: 4, core: 2. Of those that a mesh axis runs over, the one named last changes fastest.
Arguments:
- left_factors: bfloat16 [2, 2, 16384, 1536], P(None, None, 'trow', 'tcol'), may hold values from -0.15625 to 0.15625
- right_factors: bfloat16 [2, 2, 6144, 4096], P(None, None, 'tcol', 'trow'), may hold values from -0.375 to 0.375
- ranks: int32 [2, 64, 24], P(None, 'trow', 'tcol'), may hold values from 4 to 64, as said below
- v_current: float32 [2, 2, 6144, 128], P(None, None, ('tcol', 'trow')), may hold values from -32 to 32
- u_prev: float32 [2, 2, 16384, 128], P(None, None, ('trow', 'tcol')), may hold values from -32 to 32
- alpha_prev: float32 [1], replicated, may hold values from 0.5 to 2
Outputs:
- u_next: float32 [2, 2, 16384, 128], P(None, None, ('trow', 'tcol'))
- v_next: float32 [2, 2, 6144, 128], P(None, None, ('tcol', 'trow'))
- scales: float32 [2], replicated
The draws below stay inside these ranges and needn't reach their ends.
Inputs may be any that keep to these rules, and one draw needn't show every extreme that they name: `ranks`: for frequency f, tile (i, j) has rank 64 // 2 + 1 to 64 where |i * 24 - j * 64| < 192, and rank 4 to 32 elsewhere.
All inputs are finite; a program needn't handle non-finite values.
Results may differ from the reference program's by a relative error of at most 0.0028.
Values may be sent and summed in bfloat16 or wider, within the bound.
A program may use at most 128 MiB of HBM per device.

```python
import math
import jax
import jax.numpy as jnp
from jax import lax

F = 2
NV = 128
TILE = 256
RANK_MAX = 64
MT = 64
NT = 24
M = 16384
N = 6144


def draw_ranks(key, part):
    key_high, key_low = jax.random.split(jax.random.fold_in(key, 11))
    row_index = jnp.arange(MT, dtype=jnp.int32)[:, None]
    col_index = jnp.arange(NT, dtype=jnp.int32)[None, :]
    distance = jnp.abs(row_index * NT - col_index * MT)
    nearby = distance < MT * NT // 8
    higher = jax.random.randint(key_high, (F, MT, NT), RANK_MAX // 2 + 1, RANK_MAX + 1, dtype=jnp.int32)
    lower = jax.random.randint(key_low, (F, MT, NT), 4, RANK_MAX // 2 + 1, dtype=jnp.int32)
    return jnp.where(nearby[None], higher, lower)


def rising_field(key, rows):
    position = jnp.arange(rows, dtype=jnp.float32) / rows
    values = jax.random.normal(key, (F, 2, rows, NV), jnp.float32) * jnp.exp(jnp.log(3.0) * position)[:, None]
    values = values.at[:, :, rows - 1, 0].set(32.0)
    values = values.at[:, :, rows - 1, 1].set(-32.0)
    return jnp.clip(values, -32.0, 32.0)


def draw_v_current(key, part):
    return rising_field(jax.random.fold_in(key, 21), N)


def draw_u_prev(key, part):
    return rising_field(jax.random.fold_in(key, 31), M)


def strengthened(result, rng, source, target, parts, factor):
    owner, partner = [(jnp.arange(result.shape[dim]) // (result.shape[dim] // parts)).reshape([-1 if axis == dim else 1 for axis in range(result.ndim)]) for dim in (source, target)]
    chosen = jax.random.permutation(rng, parts)[partner]
    strong = (owner == chosen) | (owner == (partner + parts // 2) % parts)
    return jnp.where(strong, factor * result, result)


def shard_levels(own_key, dims, cuts, low, high):
    factor_of, own = 1.0, jax.random.fold_in(own_key, 6)
    for axis_at, shards_of in cuts:
        heights = jnp.exp(jax.random.uniform(jax.random.fold_in(own, axis_at), (shards_of,), jnp.float32, low / len(cuts), high / len(cuts)))
        factor_of = factor_of * jnp.repeat(heights, dims[axis_at] // shards_of).reshape([-1 if axis == axis_at else 1 for axis in range(len(dims))])
    return factor_of


def heavy_noise(rng, extent, width, bound, pieces, heavy, kind=jnp.bfloat16):
    drawn = width * jax.random.normal(rng, extent, jnp.float32)
    if pieces:
        drawn = drawn * shard_levels(rng, extent, pieces, -0.22, 0.18)
    return jnp.clip(strengthened(drawn, jax.random.fold_in(rng, 3), *heavy), -bound, bound).astype(kind)


def setup_inputs(seed: int = 0) -> dict:
    keys = jax.random.split(jax.random.key(seed), 7)
    left_factors = heavy_noise(keys[0], (F, 2, M, NT * RANK_MAX), (2 * NT * RANK_MAX) ** -0.5, 0.15625, ((2, 8), (3, 4)), (3, 2, 8, 2.0))
    right_factors = heavy_noise(keys[1], (F, 2, N, MT * RANK_MAX), (2 * TILE) ** -0.5, 0.375, ((2, 4), (3, 8)), (3, 2, 8, 2.0))
    ranks = draw_ranks(jax.random.fold_in(keys[6], 71), 0)
    v_current = draw_v_current(jax.random.fold_in(keys[6], 71), 0)
    u_prev = draw_u_prev(jax.random.fold_in(keys[6], 71), 0)
    alpha_prev = jnp.clip(jnp.exp(jax.random.uniform(keys[5], (1,), jnp.float32, math.log(0.5), math.log(2.0))), 0.5, 2.0)
    return {"left_factors": left_factors, "right_factors": right_factors, "ranks": ranks, "v_current": v_current, "u_prev": u_prev, "alpha_prev": alpha_prev}


epsilon = 1e-06

def complex_product(form, a_real, a_imag, b_real, b_imag, conjugate):
    real_real = jnp.einsum(form, a_real, b_real)
    imag_imag = jnp.einsum(form, a_imag, b_imag)
    real_imag = jnp.einsum(form, a_real, b_imag)
    imag_real = jnp.einsum(form, a_imag, b_real)
    if conjugate:
        return (real_real + imag_imag, real_imag - imag_real)
    return (real_real - imag_imag, real_imag + imag_real)

def to_float(array):
    return lax.optimization_barrier(array.astype(jnp.bfloat16)).astype(jnp.float32)

def reference(left_factors, right_factors, ranks, v_current, u_prev, alpha_prev):
    rank_mask = (jnp.arange(RANK_MAX)[None, None, None, :] < jnp.transpose(ranks, (0, 2, 1))[..., None]).astype(jnp.float32)

    def forward(items):
        left_one, right_one, mask_one, source_one = items
        right_tiles = right_one.astype(jnp.float32).reshape(2, NT, TILE, MT, RANK_MAX)
        sources = to_float(source_one).reshape(2, NT, TILE, NV)
        proj_real, proj_imag = complex_product('cmir,cmn->cirn', right_tiles[0], right_tiles[1], sources[0], sources[1], True)
        weight = mask_one[..., None]
        proj_real = to_float(proj_real * weight)
        proj_imag = to_float(proj_imag * weight)
        left_tiles = left_one.astype(jnp.float32).reshape(2, MT, TILE, NT, RANK_MAX)
        out_real, out_imag = complex_product('imcr,cirn->imn', left_tiles[0], left_tiles[1], proj_real, proj_imag, False)
        return jnp.stack([out_real, out_imag], 0).reshape(2, M, NV)
    image = lax.map(forward, (left_factors, right_factors, rank_mask, v_current))
    residual_u = image - alpha_prev[0] * u_prev
    beta_scale = jnp.sqrt(jnp.mean(residual_u * residual_u) + epsilon)
    u_next = residual_u / beta_scale

    def adjoint(items):
        left_one, right_one, mask_one, target_one = items
        left_tiles = left_one.astype(jnp.float32).reshape(2, MT, TILE, NT, RANK_MAX)
        targets = to_float(target_one).reshape(2, MT, TILE, NV)
        back_real, back_imag = complex_product('imcr,imn->cirn', left_tiles[0], left_tiles[1], targets[0], targets[1], True)
        weight = mask_one[..., None]
        back_real = to_float(back_real * weight)
        back_imag = to_float(back_imag * weight)
        right_tiles = right_one.astype(jnp.float32).reshape(2, NT, TILE, MT, RANK_MAX)
        out_real, out_imag = complex_product('cmir,cirn->cmn', right_tiles[0], right_tiles[1], back_real, back_imag, False)
        return jnp.stack([out_real, out_imag], 0).reshape(2, N, NV)
    image_back = lax.map(adjoint, (left_factors, right_factors, rank_mask, u_next))
    residual_v = image_back - beta_scale * v_current
    alpha_next = jnp.sqrt(jnp.mean(residual_v * residual_v) + epsilon)
    v_next = residual_v / alpha_next
    return (u_next, v_next, jnp.stack([beta_scale, alpha_next]))
```

```python
import functools
import math

import jax
import jax.numpy as jnp
from jax import lax
from jax.experimental import pallas as pl
from jax.experimental.pallas import tpu as pltpu
from jax.sharding import PartitionSpec as P

epsilon = 1e-06
MESH = pl.DeviceIdType.MESH
BF16 = jnp.bfloat16
F32 = jnp.float32


def kernel(
    R, C,
    left_hbm, right_hbm, ranks, v_cur, u_prev_hbm, alpha_prev,
    u_next, v_next, scales,
    left, right, u_prev, sslot, sfull, proj, part, back, vfull,
    rbuf, lbuf, tbuf, vsend, vrecv, norm_r, norm_c,
    load_sem, gs_sem, gr_sem, rs_sem, rr_sem, ls_sem, lr_sem,
    tr_sem, tl_sem, tt_sem, vs_sem, vr_sem, nrs_sem, nrr_sem, ncs_sem, ncr_sem,
):
    F, _, MTl, NTl = (left.shape[0], 2, ranks.shape[1], ranks.shape[2])
    rows_u, rows_v = left.shape[2], right.shape[2]
    T = rows_u // MTl
    K = left.shape[3] // NTl
    KR, KL = MTl * K, NTl * K
    ur, sr, nv = u_prev.shape[2], v_cur.shape[2], v_cur.shape[3]
    tiles = ur // T
    n = int(math.log2(R))
    r = lax.axis_index("trow")
    c = lax.axis_index("tcol")

    orders = ([0] + list(range(n - 1, 0, -1)), [0] + list(range(1, n)))

    def flip(bit):
        return (1 - 2 * ((r // 2**bit) % 2)) * 2**bit

    def owner(p, q):
        b = r
        for k in range(n):
            if (q >> (n - 1 - k)) & 1:
                b = b + flip(orders[p][k])
        return b

    def rows_of(p, q):
        return pl.ds(pl.multiple_of(owner(p, q) * sr, sr), sr)

    def tile_rows(i):
        return pl.ds(pl.multiple_of(i * T, T), T)

    def to(row, col):
        return (row, col)

    def remote(src, dst, ssem, rsem, dev):
        return pltpu.make_async_remote_copy(
            src_ref=src, dst_ref=dst, send_sem=ssem, recv_sem=rsem, device_id=dev, device_id_type=MESH
        )

    barrier = pltpu.get_barrier_semaphore()
    for d in range(1, R):
        pl.semaphore_signal(barrier, inc=1, device_id=to(lax.rem(r + d, R), c), device_id_type=MESH)
    for d in range(1, C):
        pl.semaphore_signal(barrier, inc=1, device_id=to(r, lax.rem(c + d, C)), device_id_type=MESH)

    loads = []
    for f in range(F):
        loads.append(
            (
                pltpu.make_async_copy(right_hbm.at[f], right.at[f], load_sem.at[2 * f]),
                pltpu.make_async_copy(left_hbm.at[f], left.at[f], load_sem.at[2 * f + 1]),
            )
        )
    load_u = pltpu.make_async_copy(u_prev_hbm, u_prev, load_sem.at[2 * F])
    for f in range(F):
        loads[f][0].start()
        loads[f][1].start()
    load_u.start()
    for f in range(F):
        for p in range(2):
            sslot[f, p, 0] = v_cur[f, p].astype(BF16)
    pl.semaphore_wait(barrier, R + C - 2)

    def gather_copy(f, p, m):
        bit = orders[p][n - 1 - m]
        size = 2**m
        return remote(
            sslot.at[f, p, pl.ds(0, size)], sslot.at[f, p, pl.ds(size, size)],
            gs_sem.at[f, p, m], gr_sem.at[f, p, m], to(r + flip(bit), c),
        )

    def gather_start(f, m):
        for p in range(2):
            gather_copy(f, p, m).start()

    def gather_wait(f, m):
        for p in range(2):
            gather_copy(f, p, m).wait()

    def project(f):
        for p in range(2):
            for q in range(R):
                sfull[p, rows_of(p, q), :] = sslot[f, p, q]

        def step(j, carry):
            rows = tile_rows(j)
            s_real, s_imag = sfull[0, rows, :], sfull[1, rows, :]
            weights = jnp.concatenate(
                [
                    jnp.concatenate([s_real, s_imag], 1),
                    jnp.concatenate([s_imag, -s_real], 1),
                ],
                0,
            )
            factors = jnp.concatenate([right[f, 0, rows, :], right[f, 1, rows, :]], 0)
            value = lax.dot_general(factors, weights, (((0,), (0,)), ((), ())), preferred_element_type=F32)
            index = lax.broadcasted_iota(jnp.int32, (K, 2 * nv), 0)
            for i in range(MTl):
                kept = jnp.where(index < ranks[f, i, j], value[i * K : (i + 1) * K], 0.0)
                turned = jnp.concatenate([-kept[:, nv:], kept[:, :nv]], 1)
                proj[i, pl.ds(pl.multiple_of(j * K, K), K), :] = kept.astype(BF16)
                proj[i, pl.ds(pl.multiple_of(KL + j * K, K), K), :] = turned.astype(BF16)
            return carry

        lax.fori_loop(0, NTl, step, 0)

    def image_block(f, b):
        def step(t, carry):
            i = b * tiles + t
            rows = tile_rows(i)
            factors = jnp.concatenate([left[f, 0, rows, :], left[f, 1, rows, :]], 1)
            part[f, rows, :] = jnp.dot(factors, proj[i], preferred_element_type=F32)
            return carry

        lax.fori_loop(0, tiles, step, 0)

    def block_rows(b):
        return pl.ds(pl.multiple_of(b * ur, ur), ur)

    def right_copy(f, b):
        return remote(rbuf.at[f, b], rbuf.at[f, b], rs_sem.at[f, b], rr_sem.at[f, b], to(r, lax.rem(c + 1, C)))

    def left_copy(f, b):
        return remote(lbuf.at[f, b], lbuf.at[f, b], ls_sem.at[f, b], lr_sem.at[f, b], to(r, lax.rem(c + C - 1, C)))

    def images(f):
        def step(s, carry):
            b = jnp.where(c < C // 2, C - 1 - s, s)
            image_block(f, b)

            @pl.when((c == 0) & (b > 0))
            def _():
                for p in range(2):
                    rbuf[f, b, p] = part[f, block_rows(b), p * nv : (p + 1) * nv].astype(BF16)
                right_copy(f, b).start()

            @pl.when((c == C - 1) & (b < C - 1))
            def _():
                for p in range(2):
                    lbuf[f, b, p] = part[f, block_rows(b), p * nv : (p + 1) * nv].astype(BF16)
                left_copy(f, b).start()

            return carry

        lax.fori_loop(0, C, step, 0)

    def pass_sums(f, s):
        b = C - 1 - s

        @pl.when((c > 0) & (c < b))
        def _():
            right_copy(f, b).wait_recv()
            for p in range(2):
                rbuf[f, b, p] = (
                    rbuf[f, b, p].astype(F32) + part[f, block_rows(b), p * nv : (p + 1) * nv]
                ).astype(BF16)
            right_copy(f, b).start()

        @pl.when((c > s) & (c < C - 1))
        def _():
            left_copy(f, s).wait_recv()
            for p in range(2):
                lbuf[f, s, p] = (
                    lbuf[f, s, p].astype(F32) + part[f, block_rows(s), p * nv : (p + 1) * nv]
                ).astype(BF16)
            left_copy(f, s).start()

    def give_right(f, b):
        return remote(tbuf.at[f, b], tbuf.at[f, b], tr_sem.at[f, b], tt_sem.at[f, b], to(r, lax.rem(c + 1, C)))

    def give_left(f, b):
        return remote(tbuf.at[f, b], tbuf.at[f, b], tl_sem.at[f, b], tt_sem.at[f, b], to(r, lax.rem(c + C - 1, C)))

    def squares(value):
        return jnp.sum((value * value).reshape(-1, 8, nv), axis=0)

    def finish_sums(f, total):
        @pl.when(c > 0)
        def _():
            right_copy(f, c).wait_recv()
            for p in range(2):
                lanes = slice(p * nv, (p + 1) * nv)
                part[f, block_rows(c), lanes] = part[f, block_rows(c), lanes] + rbuf[f, c, p].astype(F32)

        @pl.when(c < C - 1)
        def _():
            left_copy(f, c).wait_recv()
            for p in range(2):
                lanes = slice(p * nv, (p + 1) * nv)
                part[f, block_rows(c), lanes] = part[f, block_rows(c), lanes] + lbuf[f, c, p].astype(F32)

        for p in range(2):
            value = part[f, block_rows(c), p * nv : (p + 1) * nv] - alpha_prev[0] * u_prev[f, p]
            u_next[f, p] = value
            tbuf[f, c, p] = value.astype(BF16)
            total = total + squares(value)

        @pl.when(c < C - 1)
        def _():
            give_right(f, c).start()

        @pl.when(c > 0)
        def _():
            give_left(f, c).start()

        return total

    def pass_targets(f, s, then):
        @pl.when(c >= s)
        def _():
            b = c - s
            give_right(f, b).wait_recv()

            @pl.when(c < C - 1)
            def _():
                give_right(f, b).start()

            then(b)

        @pl.when(c + s < C)
        def _():
            b = c + s
            give_left(f, b).wait_recv()

            @pl.when(c > 0)
            def _():
                give_left(f, b).start()

            then(b)

    def norm_row(e, d):
        other = lax.rem(r + d, R)
        return remote(norm_r.at[e, r], norm_r.at[e, r], nrs_sem.at[e, d], nrr_sem.at[e, r], to(other, c))

    def norm_row_in(e, d):
        other = lax.rem(r + d, R)
        return remote(norm_r.at[e, other], norm_r.at[e, other], nrs_sem.at[e, d], nrr_sem.at[e, other], to(other, c))

    def norm_col(e, d):
        other = lax.rem(c + d, C)
        return remote(norm_c.at[e, c], norm_c.at[e, c], ncs_sem.at[e, d], ncr_sem.at[e, c], to(r, other))

    def norm_col_in(e, d):
        other = lax.rem(c + d, C)
        return remote(norm_c.at[e, other], norm_c.at[e, other], ncs_sem.at[e, d], ncr_sem.at[e, other], to(r, other))

    def norm_start(e, total):
        norm_r[e, r] = total
        for d in range(1, R):
            norm_row(e, d).start()

    def norm_finish(e, count):
        for d in range(1, R):
            norm_row_in(e, d).wait_recv()
        row_total = norm_r[e, 0]
        for d in range(1, R):
            row_total = row_total + norm_r[e, d]
        norm_c[e, c] = row_total
        for d in range(1, C):
            norm_col(e, d).start()
        for d in range(1, C):
            norm_col_in(e, d).wait_recv()
        total = norm_c[e, 0]
        for d in range(1, C):
            total = total + norm_c[e, d]
        return jnp.sqrt(jnp.sum(total, keepdims=True) / count + epsilon)

    def back_block(f, inverse):
        def run(b):
            def step(t, carry):
                i = b * tiles + t
                rows = tile_rows(i)
                inner = tile_rows(t)
                t_real, t_imag = tbuf[f, b, 0, inner, :], tbuf[f, b, 1, inner, :]
                weights = jnp.concatenate(
                    [
                        jnp.concatenate([t_real, t_imag], 1),
                        jnp.concatenate([t_imag, -t_real], 1),
                    ],
                    0,
                )
                factors = jnp.concatenate([left[f, 0, rows, :], left[f, 1, rows, :]], 0)
                value = lax.dot_general(factors, weights, (((0,), (0,)), ((), ())), preferred_element_type=F32)
                value = value * inverse
                index = lax.broadcasted_iota(jnp.int32, (K, 2 * nv), 0)
                for j in range(NTl):
                    kept = jnp.where(index < ranks[f, i, j], value[j * K : (j + 1) * K], 0.0)
                    turned = jnp.concatenate([-kept[:, nv:], kept[:, :nv]], 1)
                    back[j, pl.ds(pl.multiple_of(i * K, K), K), :] = kept.astype(BF16)
                    back[j, pl.ds(pl.multiple_of(KR + i * K, K), K), :] = turned.astype(BF16)
                return carry

            lax.fori_loop(0, tiles, step, 0)

        return run

    def back_image(f):
        def step(j, carry):
            rows = tile_rows(j)
            factors = jnp.concatenate([right[f, 0, rows, :], right[f, 1, rows, :]], 1)
            vfull[f, rows, :] = jnp.dot(factors, back[j], preferred_element_type=F32)
            return carry

        lax.fori_loop(0, NTl, step, 0)

    def halve_copy(f, p, k):
        half = R >> (k + 1)
        return remote(
            vsend.at[f, p, pl.ds(half, half)], vrecv.at[f, p, pl.ds(half, half)],
            vs_sem.at[f, p, k], vr_sem.at[f, p, k], to(r + flip(orders[p][k]), c),
        )

    def halve_start(f, k):
        half = R >> (k + 1)
        for p in range(2):
            for q in range(half, 2 * half):
                vsend[f, p, q] = vfull[f, rows_of(p, q), p * nv : (p + 1) * nv]
            halve_copy(f, p, k).start()

    def halve_wait(f, k):
        half = R >> (k + 1)
        for p in range(2):
            halve_copy(f, p, k).wait_recv()
            lanes = slice(p * nv, (p + 1) * nv)
            for q in range(half):
                rows = rows_of(p, q)
                vfull[f, rows, lanes] = vfull[f, rows, lanes] + vrecv[f, p, half + q]

    def halve_next(f, k):
        halve_wait(f, k)
        if k + 1 < n:
            halve_start(f, k + 1)

    for m in range(n):
        gather_start(0, m)
        gather_wait(0, m)
    for f in range(F):
        if f + 1 < F:
            gather_start(f + 1, 0)
        loads[f][0].wait()
        project(f)
        if f + 1 < F:
            gather_wait(f + 1, 0)
            gather_start(f + 1, 1)
        loads[f][1].wait()
        images(f)
        if f + 1 < F:
            for m in range(1, n):
                if m > 1:
                    gather_start(f + 1, m)
                gather_wait(f + 1, m)
    load_u.wait()
    nothing = lambda b: None
    total = jnp.zeros((8, nv), F32)
    for f in range(F):
        for s in range(C - 1):
            pass_sums(f, s)
            if f > 0:
                pass_targets(f - 1, s + 1, nothing)
        total = finish_sums(f, total)
    norm_start(0, total)
    count_u = F * 2 * ur * nv * R * C
    beta = norm_finish(0, count_u)
    inverse = 1.0 / beta

    for f in range(F):
        run = back_block(f, inverse)
        if f < F - 1:
            lax.fori_loop(0, C, lambda b, carry: (run(b), carry)[1], 0)
        else:
            run(c)
            for s in range(1, C):
                pass_targets(f, s, run)
                if f > 0 and s < n:
                    halve_next(f - 1, s - 1)
            if f > 0:
                for k in range(min(C - 1, n - 1), n):
                    halve_next(f - 1, k)
        back_image(f)
        halve_start(f, 0)
    for k in range(n):
        halve_next(F - 1, k)
    total = jnp.zeros((8, nv), F32)
    for f in range(F):
        for p in range(2):
            value = vfull[f, rows_of(p, 0), p * nv : (p + 1) * nv] - beta * v_cur[f, p]
            v_next[f, p] = value
            total = total + squares(value)
    norm_start(1, total)
    for f in range(F):
        for p in range(2):
            u_next[f, p] = u_next[f, p] / beta
    alpha = norm_finish(1, F * 2 * sr * nv * R * C)
    for f in range(F):
        for p in range(2):
            v_next[f, p] = v_next[f, p] / alpha
    scales[0] = beta[0, 0]
    scales[1] = alpha[0, 0]

    for f in range(F):
        for s in range(C):

            @pl.when(c < s)
            def _():
                right_copy(f, s).wait_send()

            @pl.when(c > s)
            def _():
                left_copy(f, s).wait_send()

            @pl.when((s <= c) & (c < C - 1))
            def _():
                give_right(f, s).wait_send()

            @pl.when((s >= c) & (c > 0))
            def _():
                give_left(f, s).wait_send()

        for p in range(2):
            for k in range(n):
                halve_copy(f, p, k).wait_send()
    for e in range(2):
        for d in range(1, R):
            norm_row(e, d).wait_send()
        for d in range(1, C):
            norm_col(e, d).wait_send()


def body(R, C, left_factors, right_factors, ranks, v_current, u_prev, alpha_prev):
    F, _, rows_u, KL = left_factors.shape
    rows_v, KR = right_factors.shape[2:]
    MTl, NTl = ranks.shape[1:]
    sr, nv = v_current.shape[2:]
    ur = u_prev.shape[2]
    n = int(math.log2(R))
    dma = pltpu.SemaphoreType.DMA
    anywhere = pl.BlockSpec(memory_space=pl.ANY)
    vmem = pl.BlockSpec(memory_space=pltpu.VMEM)
    smem = pl.BlockSpec(memory_space=pltpu.SMEM)
    flops = 8 * 2 * F * nv * rows_u * KL * 2
    return pl.pallas_call(
        functools.partial(kernel, R, C),
        out_shape=(
            jax.ShapeDtypeStruct(u_prev.shape, F32),
            jax.ShapeDtypeStruct(v_current.shape, F32),
            jax.ShapeDtypeStruct((2,), F32),
        ),
        in_specs=[anywhere, anywhere, smem, vmem, anywhere, smem],
        out_specs=(vmem, vmem, smem),
        scratch_shapes=[
            pltpu.VMEM(left_factors.shape, BF16),
            pltpu.VMEM(right_factors.shape, BF16),
            pltpu.VMEM(u_prev.shape, F32),
            pltpu.VMEM((F, 2, R, sr, nv), BF16),
            pltpu.VMEM((2, rows_v, nv), BF16),
            pltpu.VMEM((MTl, 2 * KL, 2 * nv), BF16),
            pltpu.VMEM((F, rows_u, 2 * nv), F32),
            pltpu.VMEM((NTl, 2 * KR, 2 * nv), BF16),
            pltpu.VMEM((F, rows_v, 2 * nv), F32),
            pltpu.VMEM((F, C, 2, ur, nv), BF16),
            pltpu.VMEM((F, C, 2, ur, nv), BF16),
            pltpu.VMEM((F, C, 2, ur, nv), BF16),
            pltpu.VMEM((F, 2, R, sr, nv), F32),
            pltpu.VMEM((F, 2, R, sr, nv), F32),
            pltpu.VMEM((2, R, 8, nv), F32),
            pltpu.VMEM((2, C, 8, nv), F32),
            dma((2 * F + 1,)),
            dma((F, 2, n)),
            dma((F, 2, n)),
            dma((F, C)),
            dma((F, C)),
            dma((F, C)),
            dma((F, C)),
            dma((F, C)),
            dma((F, C)),
            dma((F, C)),
            dma((F, 2, n)),
            dma((F, 2, n)),
            dma((2, R)),
            dma((2, R)),
            dma((2, C)),
            dma((2, C)),
        ],
        compiler_params=pltpu.CompilerParams(
            collective_id=0, has_side_effects=True, vmem_limit_bytes=56 * 1024 * 1024
        ),
        cost_estimate=pl.CostEstimate(flops=flops, bytes_accessed=16 * 1024 * 1024, transcendentals=0),
    )(left_factors, right_factors, ranks, v_current, u_prev, alpha_prev)


def solution(mesh):
    return jax.shard_map(
        functools.partial(body, mesh.shape["trow"], mesh.shape["tcol"]),
        mesh=mesh,
        in_specs=(
            P(None, None, "trow", "tcol"),
            P(None, None, "tcol", "trow"),
            P(None, "trow", "tcol"),
            P(None, None, ("tcol", "trow"), None),
            P(None, None, ("trow", "tcol"), None),
            P(),
        ),
        out_specs=(
            P(None, None, ("trow", "tcol"), None),
            P(None, None, ("tcol", "trow"), None),
            P(),
        ),
        check_vma=False,
    )
```

```python
import functools
import math

import jax
import jax.numpy as jnp
from jax import lax
from jax.experimental import pallas as pl
from jax.experimental.pallas import tpu as pltpu
from jax.sharding import PartitionSpec as P

epsilon = 1e-06
MESH = pl.DeviceIdType.MESH
BF16 = jnp.bfloat16
F32 = jnp.float32


def kernel(
    R, C,
    left_hbm, right_hbm, ranks, v_cur, u_prev_hbm, alpha_prev,
    u_next, v_next, scales,
    left, right, u_prev, sslot, sfull, proj, part, back, vfull,
    rbuf, lbuf, tbuf, vsend, vrecv, norm_r, norm_c,
    load_sem, gs_sem, gr_sem, rs_sem, rr_sem, ls_sem, lr_sem,
    tr_sem, tl_sem, tt_sem, vs_sem, vr_sem, nrs_sem, nrr_sem, ncs_sem, ncr_sem,
):
    F, _, MTl, NTl = (left.shape[0], 2, ranks.shape[1], ranks.shape[2])
    rows_u, rows_v = left.shape[2], right.shape[2]
    T = rows_u // MTl
    K = left.shape[3] // NTl
    KR, KL = MTl * K, NTl * K
    ur, sr, nv = u_prev.shape[2], v_cur.shape[2], v_cur.shape[3]
    tiles = ur // T
    n = int(math.log2(R))
    r = lax.axis_index("trow")
    c = lax.axis_index("tcol")

    orders = ([0] + list(range(n - 1, 0, -1)), [0] + list(range(1, n)))

    def flip(bit):
        return (1 - 2 * ((r // 2**bit) % 2)) * 2**bit

    def owner(p, q):
        b = r
        for k in range(n):
            if (q >> (n - 1 - k)) & 1:
                b = b + flip(orders[p][k])
        return b

    def rows_of(p, q):
        return pl.ds(pl.multiple_of(owner(p, q) * sr, sr), sr)

    def tile_rows(i):
        return pl.ds(pl.multiple_of(i * T, T), T)

    def to(row, col):
        return (row, col)

    def remote(src, dst, ssem, rsem, dev):
        return pltpu.make_async_remote_copy(
            src_ref=src, dst_ref=dst, send_sem=ssem, recv_sem=rsem, device_id=dev, device_id_type=MESH
        )

    barrier = pltpu.get_barrier_semaphore()
    for d in range(1, R):
        pl.semaphore_signal(barrier, inc=1, device_id=to(lax.rem(r + d, R), c), device_id_type=MESH)
    for d in range(1, C):
        pl.semaphore_signal(barrier, inc=1, device_id=to(r, lax.rem(c + d, C)), device_id_type=MESH)

    loads = []
    for f in range(F):
        loads.append(
            (
                pltpu.make_async_copy(right_hbm.at[f], right.at[f], load_sem.at[2 * f]),
                pltpu.make_async_copy(left_hbm.at[f], left.at[f], load_sem.at[2 * f + 1]),
            )
        )
    load_u = pltpu.make_async_copy(u_prev_hbm, u_prev, load_sem.at[2 * F])
    for f in range(F):
        loads[f][0].start()
        loads[f][1].start()
    load_u.start()
    for f in range(F):
        for p in range(2):
            sslot[f, p, 0] = v_cur[f, p].astype(BF16)
    pl.semaphore_wait(barrier, R + C - 2)

    def gather_copy(f, p, m):
        bit = orders[p][n - 1 - m]
        size = 2**m
        return remote(
            sslot.at[f, p, pl.ds(0, size)], sslot.at[f, p, pl.ds(size, size)],
            gs_sem.at[f, p, m], gr_sem.at[f, p, m], to(r + flip(bit), c),
        )

    def gather_start(f, m):
        for p in range(2):
            gather_copy(f, p, m).start()

    def gather_wait(f, m):
        for p in range(2):
            gather_copy(f, p, m).wait()

    def project(f):
        for p in range(2):
            for q in range(R):
                sfull[p, rows_of(p, q), :] = sslot[f, p, q]

        def step(j, carry):
            rows = tile_rows(j)
            s_real, s_imag = sfull[0, rows, :], sfull[1, rows, :]
            weights = jnp.concatenate(
                [
                    jnp.concatenate([s_real, s_imag], 1),
                    jnp.concatenate([s_imag, -s_real], 1),
                ],
                0,
            )
            factors = jnp.concatenate([right[f, 0, rows, :], right[f, 1, rows, :]], 0)
            value = lax.dot_general(factors, weights, (((0,), (0,)), ((), ())), preferred_element_type=F32)
            index = lax.broadcasted_iota(jnp.int32, (K, 2 * nv), 0)
            for i in range(MTl):
                kept = jnp.where(index < ranks[f, i, j], value[i * K : (i + 1) * K], 0.0)
                turned = jnp.concatenate([-kept[:, nv:], kept[:, :nv]], 1)
                proj[i, pl.ds(pl.multiple_of(j * K, K), K), :] = kept.astype(BF16)
                proj[i, pl.ds(pl.multiple_of(KL + j * K, K), K), :] = turned.astype(BF16)
            return carry

        lax.fori_loop(0, NTl, step, 0)

    def image_block(f, b):
        def step(t, carry):
            i = b * tiles + t
            rows = tile_rows(i)
            factors = jnp.concatenate([left[f, 0, rows, :], left[f, 1, rows, :]], 1)
            part[f, rows, :] = jnp.dot(factors, proj[i], preferred_element_type=F32)
            return carry

        lax.fori_loop(0, tiles, step, 0)

    def block_rows(b):
        return pl.ds(pl.multiple_of(b * ur, ur), ur)

    def right_copy(f, b):
        return remote(rbuf.at[f, b], rbuf.at[f, b], rs_sem.at[f, b], rr_sem.at[f, b], to(r, lax.rem(c + 1, C)))

    def left_copy(f, b):
        return remote(lbuf.at[f, b], lbuf.at[f, b], ls_sem.at[f, b], lr_sem.at[f, b], to(r, lax.rem(c + C - 1, C)))

    def fill_right(f, b):
        for p in range(2):
            rbuf[f, b, p] = part[f, block_rows(b), p * nv : (p + 1) * nv].astype(BF16)
        right_copy(f, b).start()

    def fill_left(f, b):
        for p in range(2):
            lbuf[f, b, p] = part[f, block_rows(b), p * nv : (p + 1) * nv].astype(BF16)
        left_copy(f, b).start()

    def images(f):
        def step(s, carry):
            image_block(f, jnp.where(c < C // 2, C - 1 - s, s))

            if f == 0:

                @pl.when((c == 0) & (s == 0))
                def _():
                    fill_right(0, C - 1)

                @pl.when((c == C - 1) & (s == 0))
                def _():
                    fill_left(0, 0)

            return carry

        lax.fori_loop(0, C, step, 0)

    def end_sums(f, s):
        later = f * (C - 1) + s + 1
        if later < F * (C - 1):
            f_later, s_later = divmod(later, C - 1)

            @pl.when(c == 0)
            def _():
                right_copy(f, C - 1 - s).wait_send()
                fill_right(f_later, C - 1 - s_later)

            @pl.when(c == C - 1)
            def _():
                left_copy(f, s).wait_send()
                fill_left(f_later, s_later)

    def sums_right(f, s, here):
        b = C - 1 - s

        @pl.when(here & (c > 0) & (c < b))
        def _():
            right_copy(f, b).wait_recv()
            for p in range(2):
                rbuf[f, b, p] = (
                    rbuf[f, b, p].astype(F32) + part[f, block_rows(b), p * nv : (p + 1) * nv]
                ).astype(BF16)
            right_copy(f, b).start()

    def sums_left(f, s, here):
        @pl.when(here & (c > s) & (c < C - 1))
        def _():
            left_copy(f, s).wait_recv()
            for p in range(2):
                lbuf[f, s, p] = (
                    lbuf[f, s, p].astype(F32) + part[f, block_rows(s), p * nv : (p + 1) * nv]
                ).astype(BF16)
            left_copy(f, s).start()

    def pass_sums(f, s, targets=False):
        low = c < C // 2
        high = c >= C // 2
        end_sums(f, s)
        sums_right(f, s, low)
        sums_left(f, s, high)
        if targets:
            targets_left(f - 1, s + 1, low)
            targets_right(f - 1, s + 1, high)
            targets_right(f - 1, s + 1, low)
            targets_left(f - 1, s + 1, high)
        sums_left(f, s, low)
        sums_right(f, s, high)

    def give_right(f, b):
        return remote(tbuf.at[f, b], tbuf.at[f, b], tr_sem.at[f, b], tt_sem.at[f, b], to(r, lax.rem(c + 1, C)))

    def give_left(f, b):
        return remote(tbuf.at[f, b], tbuf.at[f, b], tl_sem.at[f, b], tt_sem.at[f, b], to(r, lax.rem(c + C - 1, C)))

    def squares(value):
        return jnp.sum((value * value).reshape(-1, 8, nv), axis=0)

    def finish_sums(f, total):
        @pl.when(c > 0)
        def _():
            right_copy(f, c).wait_recv()
            for p in range(2):
                lanes = slice(p * nv, (p + 1) * nv)
                part[f, block_rows(c), lanes] = part[f, block_rows(c), lanes] + rbuf[f, c, p].astype(F32)

        @pl.when(c < C - 1)
        def _():
            left_copy(f, c).wait_recv()
            for p in range(2):
                lanes = slice(p * nv, (p + 1) * nv)
                part[f, block_rows(c), lanes] = part[f, block_rows(c), lanes] + lbuf[f, c, p].astype(F32)

        for p in range(2):
            value = part[f, block_rows(c), p * nv : (p + 1) * nv] - alpha_prev[0] * u_prev[f, p]
            u_next[f, p] = value
            tbuf[f, c, p] = value.astype(BF16)
            total = total + squares(value)

        @pl.when(c < C - 1)
        def _():
            give_right(f, c).start()

        @pl.when(c > 0)
        def _():
            give_left(f, c).start()

        return total

    def targets_right(f, s, here):
        @pl.when(here & (c >= s))
        def _():
            b = c - s
            give_right(f, b).wait_recv()

            @pl.when(c < C - 1)
            def _():
                give_right(f, b).start()

    def targets_left(f, s, here):
        @pl.when(here & (c + s < C))
        def _():
            b = c + s
            give_left(f, b).wait_recv()

            @pl.when(c > 0)
            def _():
                give_left(f, b).start()

    def pass_targets(f, s):
        targets_right(f, s, c >= 0)
        targets_left(f, s, c >= 0)

    def run_targets(s, run):
        @pl.when(c >= s)
        def _():
            run(c - s)

        @pl.when(c + s < C)
        def _():
            run(c + s)

    def norm_row(e, d):
        other = lax.rem(r + d, R)
        return remote(norm_r.at[e, r], norm_r.at[e, r], nrs_sem.at[e, d], nrr_sem.at[e, r], to(other, c))

    def norm_row_in(e, d):
        other = lax.rem(r + d, R)
        return remote(norm_r.at[e, other], norm_r.at[e, other], nrs_sem.at[e, d], nrr_sem.at[e, other], to(other, c))

    def norm_col(e, d):
        other = lax.rem(c + d, C)
        return remote(norm_c.at[e, c], norm_c.at[e, c], ncs_sem.at[e, d], ncr_sem.at[e, c], to(r, other))

    def norm_col_in(e, d):
        other = lax.rem(c + d, C)
        return remote(norm_c.at[e, other], norm_c.at[e, other], ncs_sem.at[e, d], ncr_sem.at[e, other], to(r, other))

    def norm_start(e, total):
        norm_r[e, r] = total
        for d in range(1, R):
            norm_row(e, d).start()

    def norm_finish(e, count):
        for d in range(1, R):
            norm_row_in(e, d).wait_recv()
        row_total = norm_r[e, 0]
        for d in range(1, R):
            row_total = row_total + norm_r[e, d]
        norm_c[e, c] = row_total
        for d in range(1, C):
            norm_col(e, d).start()
        for d in range(1, C):
            norm_col_in(e, d).wait_recv()
        total = norm_c[e, 0]
        for d in range(1, C):
            total = total + norm_c[e, d]
        return jnp.sqrt(jnp.sum(total, keepdims=True) / count + epsilon)

    def back_block(f, inverse):
        def run(b):
            def step(t, carry):
                i = b * tiles + t
                rows = tile_rows(i)
                inner = tile_rows(t)
                t_real, t_imag = tbuf[f, b, 0, inner, :], tbuf[f, b, 1, inner, :]
                weights = jnp.concatenate(
                    [
                        jnp.concatenate([t_real, t_imag], 1),
                        jnp.concatenate([t_imag, -t_real], 1),
                    ],
                    0,
                )
                factors = jnp.concatenate([left[f, 0, rows, :], left[f, 1, rows, :]], 0)
                value = lax.dot_general(factors, weights, (((0,), (0,)), ((), ())), preferred_element_type=F32)
                value = value * inverse
                index = lax.broadcasted_iota(jnp.int32, (K, 2 * nv), 0)
                for j in range(NTl):
                    kept = jnp.where(index < ranks[f, i, j], value[j * K : (j + 1) * K], 0.0)
                    turned = jnp.concatenate([-kept[:, nv:], kept[:, :nv]], 1)
                    back[j, pl.ds(pl.multiple_of(i * K, K), K), :] = kept.astype(BF16)
                    back[j, pl.ds(pl.multiple_of(KR + i * K, K), K), :] = turned.astype(BF16)
                return carry

            lax.fori_loop(0, tiles, step, 0)

        return run

    def back_image(f):
        def step(j, carry):
            rows = tile_rows(j)
            factors = jnp.concatenate([right[f, 0, rows, :], right[f, 1, rows, :]], 1)
            vfull[f, rows, :] = jnp.dot(factors, back[j], preferred_element_type=F32)
            return carry

        lax.fori_loop(0, NTl, step, 0)

    def halve_copy(f, p, k):
        half = R >> (k + 1)
        return remote(
            vsend.at[f, p, pl.ds(half, half)], vrecv.at[f, p, pl.ds(half, half)],
            vs_sem.at[f, p, k], vr_sem.at[f, p, k], to(r + flip(orders[p][k]), c),
        )

    def halve_start(f, k):
        half = R >> (k + 1)
        for p in range(2):
            for q in range(half, 2 * half):
                vsend[f, p, q] = vfull[f, rows_of(p, q), p * nv : (p + 1) * nv]
            halve_copy(f, p, k).start()

    def halve_wait(f, k):
        half = R >> (k + 1)
        for p in range(2):
            halve_copy(f, p, k).wait_recv()
            lanes = slice(p * nv, (p + 1) * nv)
            for q in range(half):
                rows = rows_of(p, q)
                vfull[f, rows, lanes] = vfull[f, rows, lanes] + vrecv[f, p, half + q]

    def halve_next(f, k):
        halve_wait(f, k)
        if k + 1 < n:
            halve_start(f, k + 1)

    for m in range(n):
        gather_start(0, m)
        gather_wait(0, m)
    for f in range(F):
        if f + 1 < F:
            gather_start(f + 1, 0)
        loads[f][0].wait()
        project(f)
        if f == 1:
            pass_sums(0, 0)
        if f + 1 < F:
            gather_wait(f + 1, 0)
            gather_start(f + 1, 1)
        loads[f][1].wait()
        images(f)
        if f + 1 < F:
            for m in range(1, n):
                if m > 1:
                    gather_start(f + 1, m)
                gather_wait(f + 1, m)
    load_u.wait()
    total = jnp.zeros((8, nv), F32)
    for f in range(F):
        for s in range(C - 1):
            if f > 0 or s > 0 or F == 1:
                pass_sums(f, s, f > 0)
        total = finish_sums(f, total)
    norm_start(0, total)
    count_u = F * 2 * ur * nv * R * C
    beta = norm_finish(0, count_u)
    inverse = 1.0 / beta

    last = F - 1
    run = back_block(last, inverse)
    steps = 0
    for s in range(1, C):
        pass_targets(last, s)
        if s == 1:
            for f in range(last):
                early = back_block(f, inverse)
                lax.fori_loop(0, C, lambda b, carry: (early(b), carry)[1], 0)
                back_image(f)
                halve_start(f, 0)
            run(c)
        elif steps < n:
            for f in range(last):
                halve_next(f, steps)
            steps += 1
        run_targets(s, run)
    back_image(last)
    halve_start(last, 0)
    for k in range(steps, n):
        for f in range(last):
            halve_next(f, k)
    for k in range(n):
        halve_next(last, k)
    total = jnp.zeros((8, nv), F32)
    for f in range(F):
        for p in range(2):
            value = vfull[f, rows_of(p, 0), p * nv : (p + 1) * nv] - beta * v_cur[f, p]
            v_next[f, p] = value
            total = total + squares(value)
    norm_start(1, total)
    for f in range(F):
        for p in range(2):
            u_next[f, p] = u_next[f, p] / beta
    alpha = norm_finish(1, F * 2 * sr * nv * R * C)
    for f in range(F):
        for p in range(2):
            v_next[f, p] = v_next[f, p] / alpha
    scales[0] = beta[0, 0]
    scales[1] = alpha[0, 0]

    for f in range(F):
        for s in range(C):

            right_left = (c > 0) | (f == F - 1 and s == 1)
            left_left = (c < C - 1) | (f == F - 1 and s == C - 2)

            @pl.when((c < s) & right_left)
            def _():
                right_copy(f, s).wait_send()

            @pl.when((c > s) & left_left)
            def _():
                left_copy(f, s).wait_send()

            @pl.when((s <= c) & (c < C - 1))
            def _():
                give_right(f, s).wait_send()

            @pl.when((s >= c) & (c > 0))
            def _():
                give_left(f, s).wait_send()

        for p in range(2):
            for k in range(n):
                halve_copy(f, p, k).wait_send()
    for e in range(2):
        for d in range(1, R):
            norm_row(e, d).wait_send()
        for d in range(1, C):
            norm_col(e, d).wait_send()


def body(R, C, left_factors, right_factors, ranks, v_current, u_prev, alpha_prev):
    F, _, rows_u, KL = left_factors.shape
    rows_v, KR = right_factors.shape[2:]
    MTl, NTl = ranks.shape[1:]
    sr, nv = v_current.shape[2:]
    ur = u_prev.shape[2]
    n = int(math.log2(R))
    dma = pltpu.SemaphoreType.DMA
    anywhere = pl.BlockSpec(memory_space=pl.ANY)
    vmem = pl.BlockSpec(memory_space=pltpu.VMEM)
    smem = pl.BlockSpec(memory_space=pltpu.SMEM)
    flops = 8 * 2 * F * nv * rows_u * KL * 2
    return pl.pallas_call(
        functools.partial(kernel, R, C),
        out_shape=(
            jax.ShapeDtypeStruct(u_prev.shape, F32),
            jax.ShapeDtypeStruct(v_current.shape, F32),
            jax.ShapeDtypeStruct((2,), F32),
        ),
        in_specs=[anywhere, anywhere, smem, vmem, anywhere, smem],
        out_specs=(vmem, vmem, smem),
        scratch_shapes=[
            pltpu.VMEM(left_factors.shape, BF16),
            pltpu.VMEM(right_factors.shape, BF16),
            pltpu.VMEM(u_prev.shape, F32),
            pltpu.VMEM((F, 2, R, sr, nv), BF16),
            pltpu.VMEM((2, rows_v, nv), BF16),
            pltpu.VMEM((MTl, 2 * KL, 2 * nv), BF16),
            pltpu.VMEM((F, rows_u, 2 * nv), F32),
            pltpu.VMEM((NTl, 2 * KR, 2 * nv), BF16),
            pltpu.VMEM((F, rows_v, 2 * nv), F32),
            pltpu.VMEM((F, C, 2, ur, nv), BF16),
            pltpu.VMEM((F, C, 2, ur, nv), BF16),
            pltpu.VMEM((F, C, 2, ur, nv), BF16),
            pltpu.VMEM((F, 2, R, sr, nv), F32),
            pltpu.VMEM((F, 2, R, sr, nv), F32),
            pltpu.VMEM((2, R, 8, nv), F32),
            pltpu.VMEM((2, C, 8, nv), F32),
            dma((2 * F + 1,)),
            dma((F, 2, n)),
            dma((F, 2, n)),
            dma((F, C)),
            dma((F, C)),
            dma((F, C)),
            dma((F, C)),
            dma((F, C)),
            dma((F, C)),
            dma((F, C)),
            dma((F, 2, n)),
            dma((F, 2, n)),
            dma((2, R)),
            dma((2, R)),
            dma((2, C)),
            dma((2, C)),
        ],
        compiler_params=pltpu.CompilerParams(
            collective_id=0, has_side_effects=True, vmem_limit_bytes=56 * 1024 * 1024
        ),
        cost_estimate=pl.CostEstimate(flops=flops, bytes_accessed=16 * 1024 * 1024, transcendentals=0),
    )(left_factors, right_factors, ranks, v_current, u_prev, alpha_prev)


def solution(mesh):
    return jax.shard_map(
        functools.partial(body, mesh.shape["trow"], mesh.shape["tcol"]),
        mesh=mesh,
        in_specs=(
            P(None, None, "trow", "tcol"),
            P(None, None, "tcol", "trow"),
            P(None, "trow", "tcol"),
            P(None, None, ("tcol", "trow"), None),
            P(None, None, ("trow", "tcol"), None),
            P(),
        ),
        out_specs=(
            P(None, None, ("trow", "tcol"), None),
            P(None, None, ("tcol", "trow"), None),
            P(),
        ),
        check_vma=False,
    )
```

```python
import functools
import math

import jax
import jax.numpy as jnp
from jax import lax
from jax.experimental import pallas as pl
from jax.experimental.pallas import tpu as pltpu
from jax.sharding import PartitionSpec as P

epsilon = 1e-06
MESH = pl.DeviceIdType.MESH
BF16 = jnp.bfloat16
F32 = jnp.float32


def kernel(
    R, C,
    left_hbm, right_hbm, ranks, v_cur, u_prev_hbm, alpha_prev,
    u_next, v_next, scales,
    left, right, u_prev, sslot, sfull, proj, part, back, vfull,
    rbuf, lbuf, tbuf, vsend, vrecv, norm_r, norm_c,
    load_sem, gs_sem, gr_sem, rs_sem, rr_sem, ls_sem, lr_sem,
    tr_sem, tl_sem, tt_sem, vs_sem, vr_sem, nrs_sem, nrr_sem, ncs_sem, ncr_sem,
):
    F, _, MTl, NTl = (left.shape[0], 2, ranks.shape[1], ranks.shape[2])
    rows_u, rows_v = left.shape[2], right.shape[2]
    T = rows_u // MTl
    K = left.shape[3] // NTl
    KR, KL = MTl * K, NTl * K
    ur, sr, nv = u_prev.shape[2], v_cur.shape[2], v_cur.shape[3]
    tiles = ur // T
    n = int(math.log2(R))
    r = lax.axis_index("trow")
    c = lax.axis_index("tcol")

    orders = ([0] + list(range(n - 1, 0, -1)), [0] + list(range(1, n)))

    def flip(bit):
        return (1 - 2 * ((r // 2**bit) % 2)) * 2**bit

    def owner(p, q):
        b = r
        for k in range(n):
            if (q >> (n - 1 - k)) & 1:
                b = b + flip(orders[p][k])
        return b

    def rows_of(p, q):
        return pl.ds(pl.multiple_of(owner(p, q) * sr, sr), sr)

    def tile_rows(i):
        return pl.ds(pl.multiple_of(i * T, T), T)

    def to(row, col):
        return (row, col)

    def remote(src, dst, ssem, rsem, dev):
        return pltpu.make_async_remote_copy(
            src_ref=src, dst_ref=dst, send_sem=ssem, recv_sem=rsem, device_id=dev, device_id_type=MESH
        )

    barrier = pltpu.get_barrier_semaphore()
    for d in range(1, R):
        pl.semaphore_signal(barrier, inc=1, device_id=to(lax.rem(r + d, R), c), device_id_type=MESH)
    for d in range(1, C):
        pl.semaphore_signal(barrier, inc=1, device_id=to(r, lax.rem(c + d, C)), device_id_type=MESH)

    loads = []
    for f in range(F):
        loads.append(
            (
                pltpu.make_async_copy(right_hbm.at[f], right.at[f], load_sem.at[2 * f]),
                pltpu.make_async_copy(left_hbm.at[f], left.at[f], load_sem.at[2 * f + 1]),
            )
        )
    load_u = pltpu.make_async_copy(u_prev_hbm, u_prev, load_sem.at[2 * F])
    for f in range(F):
        loads[f][0].start()
        loads[f][1].start()
    load_u.start()
    for f in range(F):
        for p in range(2):
            sslot[f, p, 0] = v_cur[f, p].astype(BF16)
    pl.semaphore_wait(barrier, R + C - 2)

    def gather_copy(f, p, m):
        bit = orders[p][n - 1 - m]
        size = 2**m
        return remote(
            sslot.at[f, p, pl.ds(0, size)], sslot.at[f, p, pl.ds(size, size)],
            gs_sem.at[f, p, m], gr_sem.at[f, p, m], to(r + flip(bit), c),
        )

    def gather_start(f, m):
        for p in range(2):
            gather_copy(f, p, m).start()

    def gather_wait(f, m):
        for p in range(2):
            gather_copy(f, p, m).wait()

    def project(f):
        for p in range(2):
            for q in range(R):
                sfull[p, rows_of(p, q), :] = sslot[f, p, q]

        def step(j, carry):
            rows = tile_rows(j)
            s_real, s_imag = sfull[0, rows, :], sfull[1, rows, :]
            weights = jnp.concatenate(
                [
                    jnp.concatenate([s_real, s_imag], 1),
                    jnp.concatenate([s_imag, -s_real], 1),
                ],
                0,
            )
            factors = jnp.concatenate([right[f, 0, rows, :], right[f, 1, rows, :]], 0)
            value = lax.dot_general(factors, weights, (((0,), (0,)), ((), ())), preferred_element_type=F32)
            index = lax.broadcasted_iota(jnp.int32, (K, 2 * nv), 0)
            for i in range(MTl):
                kept = jnp.where(index < ranks[f, i, j], value[i * K : (i + 1) * K], 0.0)
                turned = jnp.concatenate([-kept[:, nv:], kept[:, :nv]], 1)
                proj[i, pl.ds(pl.multiple_of(j * K, K), K), :] = kept.astype(BF16)
                proj[i, pl.ds(pl.multiple_of(KL + j * K, K), K), :] = turned.astype(BF16)
            return carry

        lax.fori_loop(0, NTl, step, 0)

    def image_block(f, b):
        def step(t, carry):
            i = b * tiles + t
            rows = tile_rows(i)
            factors = jnp.concatenate([left[f, 0, rows, :], left[f, 1, rows, :]], 1)
            part[f, rows, :] = jnp.dot(factors, proj[i], preferred_element_type=F32)
            return carry

        lax.fori_loop(0, tiles, step, 0)

    def block_rows(b):
        return pl.ds(pl.multiple_of(b * ur, ur), ur)

    def right_copy(f, b, p):
        here = rbuf.at[f, b, p]
        return remote(here, here, rs_sem.at[f, b, p], rr_sem.at[f, b, p], to(r, lax.rem(c + 1, C)))

    def left_copy(f, b, p):
        here = lbuf.at[f, b, p]
        return remote(here, here, ls_sem.at[f, b, p], lr_sem.at[f, b, p], to(r, lax.rem(c + C - 1, C)))

    def fill_right(f, b, p):
        rbuf[f, b, p] = part[f, block_rows(b), p * nv : (p + 1) * nv].astype(BF16)
        right_copy(f, b, p).start()

    def fill_left(f, b, p):
        lbuf[f, b, p] = part[f, block_rows(b), p * nv : (p + 1) * nv].astype(BF16)
        left_copy(f, b, p).start()

    def images(f):
        def step(s, carry):
            image_block(f, jnp.where(c < C // 2, C - 1 - s, s))

            if f == 0:

                @pl.when((c == 0) & (s == 0))
                def _():
                    for p in range(2):
                        fill_right(0, C - 1, p)

                @pl.when((c == C - 1) & (s == 0))
                def _():
                    for p in range(2):
                        fill_left(0, 0, p)

            return carry

        lax.fori_loop(0, C, step, 0)

    def end_sums(f, s):
        later = f * (C - 1) + s + 1
        if later < F * (C - 1):
            f_later, s_later = divmod(later, C - 1)

            @pl.when(c == 0)
            def _():
                for p in range(2):
                    right_copy(f, C - 1 - s, p).wait_send()
                    fill_right(f_later, C - 1 - s_later, p)

            @pl.when(c == C - 1)
            def _():
                for p in range(2):
                    left_copy(f, s, p).wait_send()
                    fill_left(f_later, s_later, p)

    def sums_right(f, s, here):
        b = C - 1 - s

        @pl.when(here & (c > 0) & (c < b))
        def _():
            for p in range(2):
                right_copy(f, b, p).wait_recv()
                rbuf[f, b, p] = (
                    rbuf[f, b, p].astype(F32) + part[f, block_rows(b), p * nv : (p + 1) * nv]
                ).astype(BF16)
                right_copy(f, b, p).start()

    def sums_left(f, s, here):
        @pl.when(here & (c > s) & (c < C - 1))
        def _():
            for p in range(2):
                left_copy(f, s, p).wait_recv()
                lbuf[f, s, p] = (
                    lbuf[f, s, p].astype(F32) + part[f, block_rows(s), p * nv : (p + 1) * nv]
                ).astype(BF16)
                left_copy(f, s, p).start()

    def pass_sums(f, s, targets=False):
        low = c < C // 2
        high = c >= C // 2
        end_sums(f, s)
        sums_right(f, s, low)
        sums_left(f, s, high)
        if targets:
            targets_left(f - 1, s + 1, low)
            targets_right(f - 1, s + 1, high)
            targets_right(f - 1, s + 1, low)
            targets_left(f - 1, s + 1, high)
        sums_left(f, s, low)
        sums_right(f, s, high)

    def give_right(f, b, p):
        here = tbuf.at[f, b, p]
        return remote(here, here, tr_sem.at[f, b, p], tt_sem.at[f, b, p], to(r, lax.rem(c + 1, C)))

    def give_left(f, b, p):
        here = tbuf.at[f, b, p]
        return remote(here, here, tl_sem.at[f, b, p], tt_sem.at[f, b, p], to(r, lax.rem(c + C - 1, C)))

    def squares(value):
        return jnp.sum((value * value).reshape(-1, 8, nv), axis=0)

    def finish_sums(f, total):
        for p in range(2):
            lanes = slice(p * nv, (p + 1) * nv)

            @pl.when(c > 0)
            def _():
                right_copy(f, c, p).wait_recv()
                part[f, block_rows(c), lanes] = part[f, block_rows(c), lanes] + rbuf[f, c, p].astype(F32)

            @pl.when(c < C - 1)
            def _():
                left_copy(f, c, p).wait_recv()
                part[f, block_rows(c), lanes] = part[f, block_rows(c), lanes] + lbuf[f, c, p].astype(F32)

            value = part[f, block_rows(c), lanes] - alpha_prev[0] * u_prev[f, p]
            u_next[f, p] = value
            tbuf[f, c, p] = value.astype(BF16)

            @pl.when(c < C - 1)
            def _():
                give_right(f, c, p).start()

            @pl.when(c > 0)
            def _():
                give_left(f, c, p).start()

            total = total + squares(value)
        return total

    def targets_right(f, s, here):
        @pl.when(here & (c >= s))
        def _():
            for p in range(2):
                give_right(f, c - s, p).wait_recv()

                @pl.when(c < C - 1)
                def _():
                    give_right(f, c - s, p).start()

    def targets_left(f, s, here):
        @pl.when(here & (c + s < C))
        def _():
            for p in range(2):
                give_left(f, c + s, p).wait_recv()

                @pl.when(c > 0)
                def _():
                    give_left(f, c + s, p).start()

    def pass_targets(f, s):
        targets_right(f, s, c >= 0)
        targets_left(f, s, c >= 0)

    def run_targets(s, run):
        @pl.when(c >= s)
        def _():
            run(c - s)

        @pl.when(c + s < C)
        def _():
            run(c + s)

    def norm_row(e, d):
        other = lax.rem(r + d, R)
        return remote(norm_r.at[e, r], norm_r.at[e, r], nrs_sem.at[e, d], nrr_sem.at[e, r], to(other, c))

    def norm_row_in(e, d):
        other = lax.rem(r + d, R)
        return remote(norm_r.at[e, other], norm_r.at[e, other], nrs_sem.at[e, d], nrr_sem.at[e, other], to(other, c))

    def norm_col(e, d):
        other = lax.rem(c + d, C)
        return remote(norm_c.at[e, c], norm_c.at[e, c], ncs_sem.at[e, d], ncr_sem.at[e, c], to(r, other))

    def norm_col_in(e, d):
        other = lax.rem(c + d, C)
        return remote(norm_c.at[e, other], norm_c.at[e, other], ncs_sem.at[e, d], ncr_sem.at[e, other], to(r, other))

    def norm_start(e, total):
        norm_r[e, r] = total
        for d in range(1, R):
            norm_row(e, d).start()

    def norm_finish(e, count):
        for d in range(1, R):
            norm_row_in(e, d).wait_recv()
        row_total = norm_r[e, 0]
        for d in range(1, R):
            row_total = row_total + norm_r[e, d]
        norm_c[e, c] = row_total
        for d in range(1, C):
            norm_col(e, d).start()
        for d in range(1, C):
            norm_col_in(e, d).wait_recv()
        total = norm_c[e, 0]
        for d in range(1, C):
            total = total + norm_c[e, d]
        return jnp.sqrt(jnp.sum(total, keepdims=True) / count + epsilon)

    def back_block(f, inverse):
        def run(b):
            def step(t, carry):
                i = b * tiles + t
                rows = tile_rows(i)
                inner = tile_rows(t)
                t_real, t_imag = tbuf[f, b, 0, inner, :], tbuf[f, b, 1, inner, :]
                weights = jnp.concatenate(
                    [
                        jnp.concatenate([t_real, t_imag], 1),
                        jnp.concatenate([t_imag, -t_real], 1),
                    ],
                    0,
                )
                factors = jnp.concatenate([left[f, 0, rows, :], left[f, 1, rows, :]], 0)
                value = lax.dot_general(factors, weights, (((0,), (0,)), ((), ())), preferred_element_type=F32)
                value = value * inverse
                index = lax.broadcasted_iota(jnp.int32, (K, 2 * nv), 0)
                for j in range(NTl):
                    kept = jnp.where(index < ranks[f, i, j], value[j * K : (j + 1) * K], 0.0)
                    turned = jnp.concatenate([-kept[:, nv:], kept[:, :nv]], 1)
                    back[j, pl.ds(pl.multiple_of(i * K, K), K), :] = kept.astype(BF16)
                    back[j, pl.ds(pl.multiple_of(KR + i * K, K), K), :] = turned.astype(BF16)
                return carry

            lax.fori_loop(0, tiles, step, 0)

        return run

    def back_image(f):
        def step(j, carry):
            rows = tile_rows(j)
            factors = jnp.concatenate([right[f, 0, rows, :], right[f, 1, rows, :]], 1)
            vfull[f, rows, :] = jnp.dot(factors, back[j], preferred_element_type=F32)
            return carry

        lax.fori_loop(0, NTl, step, 0)

    def halve_copy(f, p, k):
        half = R >> (k + 1)
        return remote(
            vsend.at[f, p, pl.ds(half, half)], vrecv.at[f, p, pl.ds(half, half)],
            vs_sem.at[f, p, k], vr_sem.at[f, p, k], to(r + flip(orders[p][k]), c),
        )

    def halve_start(f, k):
        half = R >> (k + 1)
        for p in range(2):
            for q in range(half, 2 * half):
                vsend[f, p, q] = vfull[f, rows_of(p, q), p * nv : (p + 1) * nv]
            halve_copy(f, p, k).start()

    def halve_wait(f, k):
        half = R >> (k + 1)
        for p in range(2):
            halve_copy(f, p, k).wait_recv()
            lanes = slice(p * nv, (p + 1) * nv)
            for q in range(half):
                rows = rows_of(p, q)
                vfull[f, rows, lanes] = vfull[f, rows, lanes] + vrecv[f, p, half + q]

    def halve_next(f, k):
        halve_wait(f, k)
        if k + 1 < n:
            halve_start(f, k + 1)

    for m in range(n):
        gather_start(0, m)
        gather_wait(0, m)
    for f in range(F):
        if f + 1 < F:
            gather_start(f + 1, 0)
        loads[f][0].wait()
        project(f)
        if f == 1:
            pass_sums(0, 0)
        if f + 1 < F:
            gather_wait(f + 1, 0)
            gather_start(f + 1, 1)
        loads[f][1].wait()
        images(f)
        if f + 1 < F:
            for m in range(1, n):
                if m > 1:
                    gather_start(f + 1, m)
                gather_wait(f + 1, m)
    load_u.wait()
    total = jnp.zeros((8, nv), F32)
    for f in range(F):
        for s in range(C - 1):
            if f > 0 or s > 0 or F == 1:
                pass_sums(f, s, f > 0)
        total = finish_sums(f, total)
    norm_start(0, total)
    count_u = F * 2 * ur * nv * R * C
    beta = norm_finish(0, count_u)
    inverse = 1.0 / beta

    last = F - 1
    run = back_block(last, inverse)
    steps = 0
    for s in range(1, C):
        if s != 2:
            pass_targets(last, s)
        if s == 1:
            for f in range(last):
                early = back_block(f, inverse)
                lax.fori_loop(0, C, lambda b, carry: (early(b), carry)[1], 0)
                if C > 2 and f == 0:
                    pass_targets(last, 2)
                back_image(f)
                halve_start(f, 0)
            run(c)
            run_targets(1, run)
            if C > 2:
                for f in range(last):
                    halve_next(f, 0)
                run_targets(2, run)
                steps = min(2, n)
                for f in range(last):
                    for k in range(1, steps):
                        halve_next(f, k)
        if s > 2:
            run_targets(s, run)
    back_image(last)
    halve_start(last, 0)
    for k in range(steps, n):
        for f in range(last):
            halve_next(f, k)
    for k in range(n):
        halve_next(last, k)
    total = jnp.zeros((8, nv), F32)
    for f in range(F):
        for p in range(2):
            value = vfull[f, rows_of(p, 0), p * nv : (p + 1) * nv] - beta * v_cur[f, p]
            v_next[f, p] = value
            total = total + squares(value)
    norm_start(1, total)
    for f in range(F):
        for p in range(2):
            u_next[f, p] = u_next[f, p] / beta
    alpha = norm_finish(1, F * 2 * sr * nv * R * C)
    for f in range(F):
        for p in range(2):
            v_next[f, p] = v_next[f, p] / alpha
    scales[0] = beta[0, 0]
    scales[1] = alpha[0, 0]

    for f in range(F):
        for s in range(C):

            right_left = (c > 0) | (f == F - 1 and s == 1)
            left_left = (c < C - 1) | (f == F - 1 and s == C - 2)

            @pl.when((c < s) & right_left)
            def _():
                for p in range(2):
                    right_copy(f, s, p).wait_send()

            @pl.when((c > s) & left_left)
            def _():
                for p in range(2):
                    left_copy(f, s, p).wait_send()

            @pl.when((s <= c) & (c < C - 1))
            def _():
                for p in range(2):
                    give_right(f, s, p).wait_send()

            @pl.when((s >= c) & (c > 0))
            def _():
                for p in range(2):
                    give_left(f, s, p).wait_send()

        for p in range(2):
            for k in range(n):
                halve_copy(f, p, k).wait_send()
    for e in range(2):
        for d in range(1, R):
            norm_row(e, d).wait_send()
        for d in range(1, C):
            norm_col(e, d).wait_send()


def body(R, C, left_factors, right_factors, ranks, v_current, u_prev, alpha_prev):
    F, _, rows_u, KL = left_factors.shape
    rows_v, KR = right_factors.shape[2:]
    MTl, NTl = ranks.shape[1:]
    sr, nv = v_current.shape[2:]
    ur = u_prev.shape[2]
    n = int(math.log2(R))
    dma = pltpu.SemaphoreType.DMA
    anywhere = pl.BlockSpec(memory_space=pl.ANY)
    vmem = pl.BlockSpec(memory_space=pltpu.VMEM)
    smem = pl.BlockSpec(memory_space=pltpu.SMEM)
    flops = 8 * 2 * F * nv * rows_u * KL * 2
    return pl.pallas_call(
        functools.partial(kernel, R, C),
        out_shape=(
            jax.ShapeDtypeStruct(u_prev.shape, F32),
            jax.ShapeDtypeStruct(v_current.shape, F32),
            jax.ShapeDtypeStruct((2,), F32),
        ),
        in_specs=[anywhere, anywhere, smem, vmem, anywhere, smem],
        out_specs=(vmem, vmem, smem),
        scratch_shapes=[
            pltpu.VMEM(left_factors.shape, BF16),
            pltpu.VMEM(right_factors.shape, BF16),
            pltpu.VMEM(u_prev.shape, F32),
            pltpu.VMEM((F, 2, R, sr, nv), BF16),
            pltpu.VMEM((2, rows_v, nv), BF16),
            pltpu.VMEM((MTl, 2 * KL, 2 * nv), BF16),
            pltpu.VMEM((F, rows_u, 2 * nv), F32),
            pltpu.VMEM((NTl, 2 * KR, 2 * nv), BF16),
            pltpu.VMEM((F, rows_v, 2 * nv), F32),
            pltpu.VMEM((F, C, 2, ur, nv), BF16),
            pltpu.VMEM((F, C, 2, ur, nv), BF16),
            pltpu.VMEM((F, C, 2, ur, nv), BF16),
            pltpu.VMEM((F, 2, R, sr, nv), F32),
            pltpu.VMEM((F, 2, R, sr, nv), F32),
            pltpu.VMEM((2, R, 8, nv), F32),
            pltpu.VMEM((2, C, 8, nv), F32),
            dma((2 * F + 1,)),
            dma((F, 2, n)),
            dma((F, 2, n)),
            dma((F, C, 2)),
            dma((F, C, 2)),
            dma((F, C, 2)),
            dma((F, C, 2)),
            dma((F, C, 2)),
            dma((F, C, 2)),
            dma((F, C, 2)),
            dma((F, 2, n)),
            dma((F, 2, n)),
            dma((2, R)),
            dma((2, R)),
            dma((2, C)),
            dma((2, C)),
        ],
        compiler_params=pltpu.CompilerParams(
            collective_id=0, has_side_effects=True, vmem_limit_bytes=56 * 1024 * 1024
        ),
        cost_estimate=pl.CostEstimate(flops=flops, bytes_accessed=16 * 1024 * 1024, transcendentals=0),
    )(left_factors, right_factors, ranks, v_current, u_prev, alpha_prev)


def solution(mesh):
    return jax.shard_map(
        functools.partial(body, mesh.shape["trow"], mesh.shape["tcol"]),
        mesh=mesh,
        in_specs=(
            P(None, None, "trow", "tcol"),
            P(None, None, "tcol", "trow"),
            P(None, "trow", "tcol"),
            P(None, None, ("tcol", "trow"), None),
            P(None, None, ("trow", "tcol"), None),
            P(),
        ),
        out_specs=(
            P(None, None, ("trow", "tcol"), None),
            P(None, None, ("tcol", "trow"), None),
            P(),
        ),
        check_vma=False,
    )
```

```python
import functools
import math

import jax
import jax.numpy as jnp
from jax import lax
from jax.experimental import pallas as pl
from jax.experimental.pallas import tpu as pltpu
from jax.sharding import PartitionSpec as P

epsilon = 1e-06
MESH = pl.DeviceIdType.MESH
BF16 = jnp.bfloat16
F32 = jnp.float32


def kernel(
    R, C,
    left_hbm, right_hbm, ranks, v_cur, u_prev_hbm, alpha_prev,
    u_next, v_next, scales,
    left, right, u_prev, sslot, sfull, proj, part, back, vfull,
    rbuf, lbuf, tbuf, vsend, vrecv, norm_r, norm_c,
    load_sem, gs_sem, gr_sem, rs_sem, rr_sem, ls_sem, lr_sem,
    tr_sem, tl_sem, tt_sem, vs_sem, vr_sem, nrs_sem, nrr_sem, ncs_sem, ncr_sem,
):
    F, _, MTl, NTl = (left.shape[0], 2, ranks.shape[1], ranks.shape[2])
    rows_u, rows_v = left.shape[2], right.shape[2]
    T = rows_u // MTl
    K = left.shape[3] // NTl
    KR, KL = MTl * K, NTl * K
    ur, sr, nv = u_prev.shape[2], v_cur.shape[2], v_cur.shape[3]
    tiles = ur // T
    n = int(math.log2(R))
    r = lax.axis_index("trow")
    c = lax.axis_index("tcol")

    orders = ([0] + list(range(n - 1, 0, -1)), [0] + list(range(1, n)))

    def flip(bit):
        return (1 - 2 * ((r // 2**bit) % 2)) * 2**bit

    def owner(p, q):
        b = r
        for k in range(n):
            if (q >> (n - 1 - k)) & 1:
                b = b + flip(orders[p][k])
        return b

    def rows_of(p, q):
        return pl.ds(pl.multiple_of(owner(p, q) * sr, sr), sr)

    def tile_rows(i):
        return pl.ds(pl.multiple_of(i * T, T), T)

    def to(row, col):
        return (row, col)

    def remote(src, dst, ssem, rsem, dev):
        return pltpu.make_async_remote_copy(
            src_ref=src, dst_ref=dst, send_sem=ssem, recv_sem=rsem, device_id=dev, device_id_type=MESH
        )

    barrier = pltpu.get_barrier_semaphore()
    for d in range(1, R):
        pl.semaphore_signal(barrier, inc=1, device_id=to(lax.rem(r + d, R), c), device_id_type=MESH)
    for d in range(1, C):
        pl.semaphore_signal(barrier, inc=1, device_id=to(r, lax.rem(c + d, C)), device_id_type=MESH)

    loads = []
    for f in range(F):
        loads.append(
            (
                pltpu.make_async_copy(right_hbm.at[f], right.at[f], load_sem.at[2 * f]),
                pltpu.make_async_copy(left_hbm.at[f], left.at[f], load_sem.at[2 * f + 1]),
            )
        )
    load_u = pltpu.make_async_copy(u_prev_hbm, u_prev, load_sem.at[2 * F])
    for f in range(F):
        loads[f][0].start()
        loads[f][1].start()
    load_u.start()
    for f in range(F):
        for p in range(2):
            sslot[f, p, 0] = v_cur[f, p].astype(BF16)
    pl.semaphore_wait(barrier, R + C - 2)

    def gather_copy(f, p, m):
        bit = orders[p][n - 1 - m]
        size = 2**m
        return remote(
            sslot.at[f, p, pl.ds(0, size)], sslot.at[f, p, pl.ds(size, size)],
            gs_sem.at[f, p, m], gr_sem.at[f, p, m], to(r + flip(bit), c),
        )

    def gather_start(f, m):
        for p in range(2):
            gather_copy(f, p, m).start()

    def gather_wait(f, m):
        for p in range(2):
            gather_copy(f, p, m).wait()

    def project(f):
        for p in range(2):
            for q in range(R):
                sfull[p, rows_of(p, q), :] = sslot[f, p, q]

        def step(j, carry):
            rows = tile_rows(j)
            s_real, s_imag = sfull[0, rows, :], sfull[1, rows, :]
            weights = jnp.concatenate(
                [
                    jnp.concatenate([s_real, s_imag], 1),
                    jnp.concatenate([s_imag, -s_real], 1),
                ],
                0,
            )
            factors = jnp.concatenate([right[f, 0, rows, :], right[f, 1, rows, :]], 0)
            value = lax.dot_general(factors, weights, (((0,), (0,)), ((), ())), preferred_element_type=F32)
            index = lax.broadcasted_iota(jnp.int32, (K, 2 * nv), 0)
            for i in range(MTl):
                kept = jnp.where(index < ranks[f, i, j], value[i * K : (i + 1) * K], 0.0)
                turned = jnp.concatenate([-kept[:, nv:], kept[:, :nv]], 1)
                proj[i, pl.ds(pl.multiple_of(j * K, K), K), :] = kept.astype(BF16)
                proj[i, pl.ds(pl.multiple_of(KL + j * K, K), K), :] = turned.astype(BF16)
            return carry

        lax.fori_loop(0, NTl, step, 0)

    def image_block(f, b):
        def step(t, carry):
            i = b * tiles + t
            rows = tile_rows(i)
            factors = jnp.concatenate([left[f, 0, rows, :], left[f, 1, rows, :]], 1)
            part[f, rows, :] = jnp.dot(factors, proj[i], preferred_element_type=F32)
            return carry

        lax.fori_loop(0, tiles, step, 0)

    def block_rows(b):
        return pl.ds(pl.multiple_of(b * ur, ur), ur)

    def right_copy(f, b):
        return remote(rbuf.at[f, b], rbuf.at[f, b], rs_sem.at[f, b], rr_sem.at[f, b], to(r, lax.rem(c + 1, C)))

    def left_copy(f, b):
        return remote(lbuf.at[f, b], lbuf.at[f, b], ls_sem.at[f, b], lr_sem.at[f, b], to(r, lax.rem(c + C - 1, C)))

    def fill_right(f, b):
        for p in range(2):
            rbuf[f, b, p] = part[f, block_rows(b), p * nv : (p + 1) * nv].astype(BF16)
        right_copy(f, b).start()

    def fill_left(f, b):
        for p in range(2):
            lbuf[f, b, p] = part[f, block_rows(b), p * nv : (p + 1) * nv].astype(BF16)
        left_copy(f, b).start()

    def images(f):
        def step(s, carry):
            image_block(f, jnp.where(c < C // 2, C - 1 - s, s))

            if f == 0:

                @pl.when((c == 0) & (s == 0))
                def _():
                    fill_right(0, C - 1)

                @pl.when((c == C - 1) & (s == 0))
                def _():
                    fill_left(0, 0)

            return carry

        lax.fori_loop(0, C, step, 0)

    def end_sums(f, s):
        later = f * (C - 1) + s + 1
        if later < F * (C - 1):
            f_later, s_later = divmod(later, C - 1)

            @pl.when(c == 0)
            def _():
                right_copy(f, C - 1 - s).wait_send()
                fill_right(f_later, C - 1 - s_later)

            @pl.when(c == C - 1)
            def _():
                left_copy(f, s).wait_send()
                fill_left(f_later, s_later)

    def sums_right(f, s, here):
        b = C - 1 - s

        @pl.when(here & (c > 0) & (c < b))
        def _():
            right_copy(f, b).wait_recv()
            for p in range(2):
                rbuf[f, b, p] = (
                    rbuf[f, b, p].astype(F32) + part[f, block_rows(b), p * nv : (p + 1) * nv]
                ).astype(BF16)
            right_copy(f, b).start()

    def sums_left(f, s, here):
        @pl.when(here & (c > s) & (c < C - 1))
        def _():
            left_copy(f, s).wait_recv()
            for p in range(2):
                lbuf[f, s, p] = (
                    lbuf[f, s, p].astype(F32) + part[f, block_rows(s), p * nv : (p + 1) * nv]
                ).astype(BF16)
            left_copy(f, s).start()

    def pass_sums(f, s, targets=False):
        low = c < C // 2
        high = c >= C // 2
        end_sums(f, s)
        sums_right(f, s, low)
        sums_left(f, s, high)
        if targets:
            targets_left(f - 1, s + 1, low)
            targets_right(f - 1, s + 1, high)
            targets_right(f - 1, s + 1, low)
            targets_left(f - 1, s + 1, high)
        sums_left(f, s, low)
        sums_right(f, s, high)

    def give_right(f, b):
        return remote(tbuf.at[f, b], tbuf.at[f, b], tr_sem.at[f, b], tt_sem.at[f, b], to(r, lax.rem(c + 1, C)))

    def give_left(f, b):
        return remote(tbuf.at[f, b], tbuf.at[f, b], tl_sem.at[f, b], tt_sem.at[f, b], to(r, lax.rem(c + C - 1, C)))

    def squares(value):
        return jnp.sum((value * value).reshape(-1, 8, nv), axis=0)

    def finish_sums(f, total):
        @pl.when(c > 0)
        def _():
            right_copy(f, c).wait_recv()
            for p in range(2):
                lanes = slice(p * nv, (p + 1) * nv)
                part[f, block_rows(c), lanes] = part[f, block_rows(c), lanes] + rbuf[f, c, p].astype(F32)

        @pl.when(c < C - 1)
        def _():
            left_copy(f, c).wait_recv()
            for p in range(2):
                lanes = slice(p * nv, (p + 1) * nv)
                part[f, block_rows(c), lanes] = part[f, block_rows(c), lanes] + lbuf[f, c, p].astype(F32)

        for p in range(2):
            value = part[f, block_rows(c), p * nv : (p + 1) * nv] - alpha_prev[0] * u_prev[f, p]
            u_next[f, p] = value
            tbuf[f, c, p] = value.astype(BF16)
            total = total + squares(value)

        @pl.when(c < C - 1)
        def _():
            give_right(f, c).start()

        @pl.when(c > 0)
        def _():
            give_left(f, c).start()

        return total

    def targets_right(f, s, here):
        @pl.when(here & (c >= s))
        def _():
            b = c - s
            give_right(f, b).wait_recv()

            @pl.when(c < C - 1)
            def _():
                give_right(f, b).start()

    def targets_left(f, s, here):
        @pl.when(here & (c + s < C))
        def _():
            b = c + s
            give_left(f, b).wait_recv()

            @pl.when(c > 0)
            def _():
                give_left(f, b).start()

    def pass_targets(f, s):
        targets_right(f, s, c >= 0)
        targets_left(f, s, c >= 0)

    def run_targets(s, run):
        @pl.when(c >= s)
        def _():
            run(c - s)

        @pl.when(c + s < C)
        def _():
            run(c + s)

    def norm_row(e, d):
        other = lax.rem(r + d, R)
        return remote(norm_r.at[e, r], norm_r.at[e, r], nrs_sem.at[e, d], nrr_sem.at[e, r], to(other, c))

    def norm_row_in(e, d):
        other = lax.rem(r + d, R)
        return remote(norm_r.at[e, other], norm_r.at[e, other], nrs_sem.at[e, d], nrr_sem.at[e, other], to(other, c))

    def norm_col(e, d):
        other = lax.rem(c + d, C)
        return remote(norm_c.at[e, c], norm_c.at[e, c], ncs_sem.at[e, d], ncr_sem.at[e, c], to(r, other))

    def norm_col_in(e, d):
        other = lax.rem(c + d, C)
        return remote(norm_c.at[e, other], norm_c.at[e, other], ncs_sem.at[e, d], ncr_sem.at[e, other], to(r, other))

    def norm_start(e, total):
        norm_r[e, r] = total
        for d in range(1, R):
            norm_row(e, d).start()

    def norm_finish(e, count):
        for d in range(1, R):
            norm_row_in(e, d).wait_recv()
        row_total = norm_r[e, 0]
        for d in range(1, R):
            row_total = row_total + norm_r[e, d]
        norm_c[e, c] = row_total
        for d in range(1, C):
            norm_col(e, d).start()
        for d in range(1, C):
            norm_col_in(e, d).wait_recv()
        total = norm_c[e, 0]
        for d in range(1, C):
            total = total + norm_c[e, d]
        return jnp.sqrt(jnp.sum(total, keepdims=True) / count + epsilon)

    def back_block(f, inverse):
        def run(b):
            def step(t, carry):
                i = b * tiles + t
                rows = tile_rows(i)
                inner = tile_rows(t)
                t_real, t_imag = tbuf[f, b, 0, inner, :], tbuf[f, b, 1, inner, :]
                weights = jnp.concatenate(
                    [
                        jnp.concatenate([t_real, t_imag], 1),
                        jnp.concatenate([t_imag, -t_real], 1),
                    ],
                    0,
                )
                factors = jnp.concatenate([left[f, 0, rows, :], left[f, 1, rows, :]], 0)
                value = lax.dot_general(factors, weights, (((0,), (0,)), ((), ())), preferred_element_type=F32)
                value = value * inverse
                index = lax.broadcasted_iota(jnp.int32, (K, 2 * nv), 0)
                for j in range(NTl):
                    kept = jnp.where(index < ranks[f, i, j], value[j * K : (j + 1) * K], 0.0)
                    turned = jnp.concatenate([-kept[:, nv:], kept[:, :nv]], 1)
                    back[j, pl.ds(pl.multiple_of(i * K, K), K), :] = kept.astype(BF16)
                    back[j, pl.ds(pl.multiple_of(KR + i * K, K), K), :] = turned.astype(BF16)
                return carry

            lax.fori_loop(0, tiles, step, 0)

        return run

    def back_image(f):
        def step(j, carry):
            rows = tile_rows(j)
            factors = jnp.concatenate([right[f, 0, rows, :], right[f, 1, rows, :]], 1)
            vfull[f, rows, :] = jnp.dot(factors, back[j], preferred_element_type=F32)
            return carry

        lax.fori_loop(0, NTl, step, 0)

    def halve_copy(f, p, k):
        half = R >> (k + 1)
        return remote(
            vsend.at[f, p, pl.ds(half, half)], vrecv.at[f, p, pl.ds(half, half)],
            vs_sem.at[f, p, k], vr_sem.at[f, p, k], to(r + flip(orders[p][k]), c),
        )

    def halve_start(f, k):
        half = R >> (k + 1)
        for p in range(2):
            for q in range(half, 2 * half):
                vsend[f, p, q] = vfull[f, rows_of(p, q), p * nv : (p + 1) * nv]
            halve_copy(f, p, k).start()

    def halve_wait(f, k):
        half = R >> (k + 1)
        for p in range(2):
            halve_copy(f, p, k).wait_recv()
            lanes = slice(p * nv, (p + 1) * nv)
            for q in range(half):
                rows = rows_of(p, q)
                vfull[f, rows, lanes] = vfull[f, rows, lanes] + vrecv[f, p, half + q]

    def halve_next(f, k):
        halve_wait(f, k)
        if k + 1 < n:
            halve_start(f, k + 1)

    for m in range(n):
        gather_start(0, m)
        gather_wait(0, m)
    for f in range(F):
        if f + 1 < F:
            gather_start(f + 1, 0)
        loads[f][0].wait()
        if f == 1:
            pass_sums(0, 0)
        project(f)
        if f == 1 and C > 2:
            pass_sums(0, 1)
        if f + 1 < F:
            gather_wait(f + 1, 0)
            gather_start(f + 1, 1)
        loads[f][1].wait()
        images(f)
        if f + 1 < F:
            for m in range(1, n):
                if m > 1:
                    gather_start(f + 1, m)
                gather_wait(f + 1, m)
    load_u.wait()
    total = jnp.zeros((8, nv), F32)
    for f in range(F):
        for s in range(C - 1):
            if f > 0 or s > 1 or F == 1:
                pass_sums(f, s, f > 0)
        total = finish_sums(f, total)
    norm_start(0, total)
    count_u = F * 2 * ur * nv * R * C
    beta = norm_finish(0, count_u)
    inverse = 1.0 / beta

    last = F - 1
    run = back_block(last, inverse)
    steps = 0
    for s in range(1, C):
        if s != 2:
            pass_targets(last, s)
        if s == 1:
            for f in range(last):
                early = back_block(f, inverse)
                lax.fori_loop(0, C, lambda b, carry: (early(b), carry)[1], 0)
                if C > 2 and f == 0:
                    pass_targets(last, 2)
                back_image(f)
                halve_start(f, 0)
            run(c)
            run_targets(1, run)
            if C > 2:
                for f in range(last):
                    halve_next(f, 0)
                run_targets(2, run)
                steps = min(2, n)
                for f in range(last):
                    for k in range(1, steps):
                        halve_next(f, k)
        if s > 2:
            run_targets(s, run)
    back_image(last)
    halve_start(last, 0)
    for k in range(steps, n):
        for f in range(last):
            halve_next(f, k)
    for k in range(n):
        halve_next(last, k)
    total = jnp.zeros((8, nv), F32)
    for f in range(F):
        for p in range(2):
            value = vfull[f, rows_of(p, 0), p * nv : (p + 1) * nv] - beta * v_cur[f, p]
            v_next[f, p] = value
            total = total + squares(value)
    norm_start(1, total)
    for f in range(F):
        for p in range(2):
            u_next[f, p] = u_next[f, p] / beta
    alpha = norm_finish(1, F * 2 * sr * nv * R * C)
    for f in range(F):
        for p in range(2):
            v_next[f, p] = v_next[f, p] / alpha
    scales[0] = beta[0, 0]
    scales[1] = alpha[0, 0]

    for f in range(F):
        for s in range(C):

            right_left = (c > 0) | (f == F - 1 and s == 1)
            left_left = (c < C - 1) | (f == F - 1 and s == C - 2)

            @pl.when((c < s) & right_left)
            def _():
                right_copy(f, s).wait_send()

            @pl.when((c > s) & left_left)
            def _():
                left_copy(f, s).wait_send()

            @pl.when((s <= c) & (c < C - 1))
            def _():
                give_right(f, s).wait_send()

            @pl.when((s >= c) & (c > 0))
            def _():
                give_left(f, s).wait_send()

        for p in range(2):
            for k in range(n):
                halve_copy(f, p, k).wait_send()
    for e in range(2):
        for d in range(1, R):
            norm_row(e, d).wait_send()
        for d in range(1, C):
            norm_col(e, d).wait_send()


def body(R, C, left_factors, right_factors, ranks, v_current, u_prev, alpha_prev):
    F, _, rows_u, KL = left_factors.shape
    rows_v, KR = right_factors.shape[2:]
    MTl, NTl = ranks.shape[1:]
    sr, nv = v_current.shape[2:]
    ur = u_prev.shape[2]
    n = int(math.log2(R))
    dma = pltpu.SemaphoreType.DMA
    anywhere = pl.BlockSpec(memory_space=pl.ANY)
    vmem = pl.BlockSpec(memory_space=pltpu.VMEM)
    smem = pl.BlockSpec(memory_space=pltpu.SMEM)
    flops = 8 * 2 * F * nv * rows_u * KL * 2
    return pl.pallas_call(
        functools.partial(kernel, R, C),
        out_shape=(
            jax.ShapeDtypeStruct(u_prev.shape, F32),
            jax.ShapeDtypeStruct(v_current.shape, F32),
            jax.ShapeDtypeStruct((2,), F32),
        ),
        in_specs=[anywhere, anywhere, smem, vmem, anywhere, smem],
        out_specs=(vmem, vmem, smem),
        scratch_shapes=[
            pltpu.VMEM(left_factors.shape, BF16),
            pltpu.VMEM(right_factors.shape, BF16),
            pltpu.VMEM(u_prev.shape, F32),
            pltpu.VMEM((F, 2, R, sr, nv), BF16),
            pltpu.VMEM((2, rows_v, nv), BF16),
            pltpu.VMEM((MTl, 2 * KL, 2 * nv), BF16),
            pltpu.VMEM((F, rows_u, 2 * nv), F32),
            pltpu.VMEM((NTl, 2 * KR, 2 * nv), BF16),
            pltpu.VMEM((F, rows_v, 2 * nv), F32),
            pltpu.VMEM((F, C, 2, ur, nv), BF16),
            pltpu.VMEM((F, C, 2, ur, nv), BF16),
            pltpu.VMEM((F, C, 2, ur, nv), BF16),
            pltpu.VMEM((F, 2, R, sr, nv), F32),
            pltpu.VMEM((F, 2, R, sr, nv), F32),
            pltpu.VMEM((2, R, 8, nv), F32),
            pltpu.VMEM((2, C, 8, nv), F32),
            dma((2 * F + 1,)),
            dma((F, 2, n)),
            dma((F, 2, n)),
            dma((F, C)),
            dma((F, C)),
            dma((F, C)),
            dma((F, C)),
            dma((F, C)),
            dma((F, C)),
            dma((F, C)),
            dma((F, 2, n)),
            dma((F, 2, n)),
            dma((2, R)),
            dma((2, R)),
            dma((2, C)),
            dma((2, C)),
        ],
        compiler_params=pltpu.CompilerParams(
            collective_id=0, has_side_effects=True, vmem_limit_bytes=56 * 1024 * 1024
        ),
        cost_estimate=pl.CostEstimate(flops=flops, bytes_accessed=16 * 1024 * 1024, transcendentals=0),
    )(left_factors, right_factors, ranks, v_current, u_prev, alpha_prev)


def solution(mesh):
    return jax.shard_map(
        functools.partial(body, mesh.shape["trow"], mesh.shape["tcol"]),
        mesh=mesh,
        in_specs=(
            P(None, None, "trow", "tcol"),
            P(None, None, "tcol", "trow"),
            P(None, "trow", "tcol"),
            P(None, None, ("tcol", "trow"), None),
            P(None, None, ("trow", "tcol"), None),
            P(),
        ),
        out_specs=(
            P(None, None, ("trow", "tcol"), None),
            P(None, None, ("tcol", "trow"), None),
            P(),
        ),
        check_vma=False,
    )
```
